256 devices in a mesh: ctx: 16 (over y, x), tp: 16 (over z, core).
Axes of the slice: x: 4, y: 4, z: 8, core: 2. Of those that a mesh axis runs over, the one named last changes fastest.
Arguments:
- queries: bfloat16 [8192, 16384], P(('ctx', 'tp')), may hold values from -4.5 to 4.5
- key_vectors: bfloat16 [8192, 1024], P(('ctx', 'tp')), may hold values from -5 to 5
- value_vectors: bfloat16 [8192, 1024], P(('ctx', 'tp')), may hold values from -6 to 6
- output_cotangent: bfloat16 [8192, 16384], P(('ctx', 'tp')), may hold values from -6 to 6
- doc_lengths: int32 [16], replicated, may hold values from 1 to 1025, as said below
Outputs:
- attended: bfloat16 [8192, 16384], P(('ctx', 'tp'))
- query_gradient: bfloat16 [8192, 16384], P(('ctx', 'tp'))
- key_gradient: bfloat16 [8192, 1024], P(('ctx', 'tp'))
- value_gradient: bfloat16 [8192, 1024], P(('ctx', 'tp'))
The draws below stay inside these ranges and needn't reach their ends.
Inputs may be any that keep to these rules, and one draw needn't show every extreme that they name: `doc_lengths`: the 16 lengths sum to 8192; exactly one of them equals 1025.
All inputs are finite; a program needn't handle non-finite values.
Results may differ from the reference program's by a relative error of at most 0.02.
Values may be sent and summed in bfloat16 or wider, within the bound.
No kernel may reach another device: no remote copies, remote signals or barrier semaphores. Data moves between devices by JAX's collectives and lax.ppermute only.
A program may use at most 192 MiB of HBM per device.

```python
import math
import jax
import jax.numpy as jnp
from jax import lax

TOK_DEV = 512
HEAD_DIM = 128
GROUP = 16
KV_HEADS = 8
SPAN = 2
HEADS = 128
TOKENS = 8192
NDOC = 16
DOC_MAX = 1025


def document_draw(key):
    base_key = jax.random.fold_in(key, 101)
    pick_key, weight_key = jax.random.split(base_key)
    longest = jax.random.randint(pick_key, (), 0, NDOC, dtype=jnp.int32)
    slots = jnp.arange(NDOC, dtype=jnp.int32)
    shares = jax.random.randint(weight_key, (NDOC,), 2, 5, dtype=jnp.int32)
    shares = jnp.where(slots == longest, 0, shares)
    running = jnp.cumsum(shares).astype(jnp.int32)
    spare = TOKENS - DOC_MAX - (NDOC - 1)
    marks = (spare * running // jnp.sum(shares)).astype(jnp.int32)
    earlier = jnp.concatenate([jnp.zeros((1,), jnp.int32), marks[:-1]])
    lengths = jnp.where(slots == longest, DOC_MAX, 1 + marks - earlier).astype(jnp.int32)
    return lengths


def draw_doc_lengths(key, part):
    lengths = document_draw(key)
    return lengths


def draw_queries(key, part):
    key = jax.random.fold_in(key, 7)
    values = jnp.clip(0.5 * jax.random.normal(key, (TOKENS, HEADS * HEAD_DIM), jnp.float32), -4.5, 4.5)
    return values.astype(jnp.bfloat16)


def draw_key_vectors(key, part):
    key = jax.random.fold_in(key, 11)
    scale_key, value_key = jax.random.split(key)
    row_scale = jnp.exp(jax.random.uniform(scale_key, (TOKENS, 1), jnp.float32, jnp.log(0.25), jnp.log(2.5)))
    values = jnp.clip(jax.random.normal(value_key, (TOKENS, KV_HEADS * HEAD_DIM), jnp.float32) * row_scale, -5.0, 5.0)
    return values.astype(jnp.bfloat16)


def level_of(stream_key, extent, cuts, smallest, largest):
    def one(position, parts):
        heights = jax.random.uniform(jax.random.fold_in(jax.random.fold_in(stream_key, 6), position), (parts,), jnp.float32, smallest / len(cuts), largest / len(cuts))
        return jnp.repeat(jnp.exp(heights), extent[position] // parts).reshape((-1,) + (1,) * (len(extent) - position - 1))

    loudness = one(*cuts[0])
    for cut in cuts[1:]:
        loudness = loudness * one(*cut)
    return loudness


def noise(stream_key, dims, deviation, bound, pieces=(), kind=jnp.bfloat16):
    gain = level_of(stream_key, dims, pieces, -0.22, 0.18) if pieces else 1.0
    values = jax.random.normal(stream_key, dims, jnp.float32) * deviation * gain
    return jnp.minimum(jnp.maximum(values, -bound), bound).astype(kind)


def setup_inputs(seed: int = 0) -> dict:
    streams_of = jax.random.split(jax.random.key(seed), 6)
    queries = draw_queries(jax.random.fold_in(streams_of[5], 71), 0)
    key_vectors = draw_key_vectors(jax.random.fold_in(streams_of[5], 71), 0)
    value_vectors = noise(streams_of[2], (TOKENS, KV_HEADS * HEAD_DIM), 1.0, 6.0, ((0, 256),))
    output_cotangent = noise(streams_of[3], (TOKENS, HEADS * HEAD_DIM), 1.0, 6.0, ((0, 256),))
    doc_lengths = draw_doc_lengths(jax.random.fold_in(streams_of[5], 71), 0)
    return {"queries": queries, "key_vectors": key_vectors, "value_vectors": value_vectors, "output_cotangent": output_cotangent, "doc_lengths": doc_lengths}


def document_ids(positions, doc_lengths):
    endings = jnp.cumsum(doc_lengths).astype(jnp.int32)
    passed = lax.optimization_barrier(jnp.sum((positions[:, None] >= endings[None, :]).astype(jnp.int32), axis=1))
    return jnp.where(positions >= 0, passed, -1).astype(jnp.int32)

def reference(queries, key_vectors, value_vectors, output_cotangent, doc_lengths):
    softmax_scale = 1.0 / math.sqrt(HEAD_DIM)
    block_rows = min(128, TOK_DEV)
    reach_rows = SPAN * TOK_DEV
    window = reach_rows + block_rows
    padding = jnp.zeros((reach_rows, KV_HEADS * HEAD_DIM), jnp.bfloat16)
    padded_keys = jnp.concatenate([padding, key_vectors], axis=0)
    padded_values = jnp.concatenate([padding, value_vectors], axis=0)
    all_ids = document_ids(jnp.arange(-reach_rows, TOKENS, dtype=jnp.int32), doc_lengths)

    def advance(totals, number):
        key_total, value_total = totals
        first_row = (number * block_rows).astype(jnp.int32)
        query_block = lax.dynamic_slice_in_dim(queries, first_row, block_rows, 0).astype(jnp.float32).reshape(block_rows, KV_HEADS, GROUP, HEAD_DIM)
        slope_block = lax.dynamic_slice_in_dim(output_cotangent, first_row, block_rows, 0).astype(jnp.float32).reshape(block_rows, KV_HEADS, GROUP, HEAD_DIM)
        key_block = lax.dynamic_slice_in_dim(padded_keys, first_row, window, 0).astype(jnp.float32).reshape(window, KV_HEADS, HEAD_DIM)
        value_block = lax.dynamic_slice_in_dim(padded_values, first_row, window, 0).astype(jnp.float32).reshape(window, KV_HEADS, HEAD_DIM)
        key_ids = lax.dynamic_slice_in_dim(all_ids, first_row, window, 0)
        query_ids = key_ids[reach_rows:]
        key_positions = first_row - reach_rows + jnp.arange(window, dtype=jnp.int32)
        query_positions = first_row + jnp.arange(block_rows, dtype=jnp.int32)
        allowed = (query_ids[:, None] == key_ids[None, :]) & (key_positions[None, :] <= query_positions[:, None])
        scores = jnp.einsum('igrd,jgd->grij', query_block, key_block) * softmax_scale
        masked = jnp.where(allowed, scores, -1e+30)
        highest = lax.optimization_barrier(jnp.max(masked, axis=-1, keepdims=True))
        row_total = lax.optimization_barrier(jnp.sum(jnp.where(allowed, jnp.exp(masked - highest), 0.0), axis=-1, keepdims=True))
        log_total = highest + jnp.log(row_total)
        probabilities = jnp.where(allowed, jnp.exp(masked - log_total), 0.0)
        weights_low = probabilities.astype(jnp.bfloat16)
        weights_back = lax.optimization_barrier(weights_low).astype(jnp.float32)
        attended = jnp.einsum('grij,jgd->igrd', weights_back, value_block)
        attended_low = attended.astype(jnp.bfloat16)
        attended_back = lax.optimization_barrier(attended_low).astype(jnp.float32)
        deltas = lax.optimization_barrier(jnp.sum(slope_block * attended_back, axis=-1))
        weight_slopes = jnp.einsum('igrd,jgd->grij', slope_block, value_block)
        score_slopes = probabilities * (weight_slopes - jnp.transpose(deltas, (1, 2, 0))[..., None])
        slopes_low = score_slopes.astype(jnp.bfloat16)
        slopes_back = lax.optimization_barrier(slopes_low).astype(jnp.float32)
        query_slope = (jnp.einsum('grij,jgd->igrd', slopes_back, key_block) * softmax_scale).astype(jnp.bfloat16)
        key_part = jnp.einsum('grij,igrd->jgd', slopes_back, query_block) * softmax_scale
        value_part = jnp.einsum('grij,igrd->jgd', weights_back, slope_block)
        key_total = lax.dynamic_update_slice_in_dim(key_total, lax.dynamic_slice_in_dim(key_total, first_row, window, 0) + key_part, first_row, 0)
        value_total = lax.dynamic_update_slice_in_dim(value_total, lax.dynamic_slice_in_dim(value_total, first_row, window, 0) + value_part, first_row, 0)
        return ((key_total, value_total), (attended_low.reshape(block_rows, HEADS * HEAD_DIM), query_slope.reshape(block_rows, HEADS * HEAD_DIM)))
    starting = jnp.zeros((reach_rows + TOKENS, KV_HEADS, HEAD_DIM), jnp.float32)
    totals, stacked = lax.scan(advance, (starting, starting), jnp.arange(TOKENS // block_rows, dtype=jnp.int32))
    attended_all = stacked[0].reshape(TOKENS, HEADS * HEAD_DIM)
    query_all = stacked[1].reshape(TOKENS, HEADS * HEAD_DIM)
    key_all = totals[0][reach_rows:].reshape(TOKENS, KV_HEADS * HEAD_DIM).astype(jnp.bfloat16)
    value_all = totals[1][reach_rows:].reshape(TOKENS, KV_HEADS * HEAD_DIM).astype(jnp.bfloat16)
    return (attended_all, query_all, key_all, value_all)
```

```python
import functools
import math

import jax
import jax.numpy as jnp
from jax import lax
from jax.experimental import pallas as pl
from jax.experimental.pallas import tpu as pltpu
from jax.sharding import Mesh, PartitionSpec as P

HEAD_DIM = 128
KV_HEADS = 8
GROUP = 16
NDOC = 16
CHUNK = 64
RING = 8
ROW = 4
UNITS = ROW + 2
REACH = 16
WINDOW = (REACH + 1) * CHUNK
CLASSES = (17, 12, 8, 4)
HEADS_STEP = 4
ROWS_STEP = HEADS_STEP * CHUNK
MASK_FILL = -1e30
SCALE = 1.0 / math.sqrt(HEAD_DIM)
SCALE_LOG2 = SCALE * math.log2(math.e)
BF16 = jnp.bfloat16
F32 = jnp.float32
HEAD_AXES = ("x", "core")
WIDE = GROUP * HEAD_DIM


def dot_t(a, b):
    return lax.dot_general(a, b, (((1,), (1,)), ((), ())), preferred_element_type=F32)


def dot(a, b):
    return jnp.dot(a, b, preferred_element_type=F32)


def attention_kernel(place, lengths, qdo_ref, *refs):
    kv_refs = refs[:RING]
    v4_ref = refs[RING]
    odq_ref = refs[RING + 1]
    dkv_refs = refs[RING + 2 : 2 * RING + 2]
    dv4_ref = refs[2 * RING + 2]
    kwin, vwin, dwin, acc = refs[2 * RING + 3 :]
    step = pl.program_id(0)
    z = place[1]
    first = ((place[0] * ROW + step) * RING + z) * CHUNK
    base = first - REACH * CHUNK

    @pl.when(step == 0)
    def _():
        acc[...] = jnp.zeros_like(acc)

    def unit(t):
        return step + t // RING + (z + t % RING >= RING).astype(jnp.int32)

    tokens = first + lax.broadcasted_iota(jnp.int32, (CHUNK, 1), 0)
    starts = jnp.zeros((CHUNK, 1), jnp.int32)
    ending = jnp.int32(0)
    earliest = jnp.int32(0)
    for d in range(NDOC):
        ending = ending + lengths[d]
        starts = jnp.where(tokens >= ending, ending, starts)
        earliest = jnp.where(first >= ending, ending, earliest)
    needed = REACH + 1 - (earliest - base) // CHUNK

    def run(chunks):
        skipped = REACH + 1 - chunks
        width = chunks * CHUNK
        for t in range(skipped, REACH + 1):
            at = (t - skipped) * CHUNK
            slot = t % RING
            if slot == RING // 2:
                kwin[at : at + CHUNK, :] = kv_refs[slot][unit(t)]
                vwin[at : at + CHUNK, :] = v4_ref[unit(t)]
            else:
                pair = kv_refs[slot][unit(t)]
                kwin[at : at + CHUNK, :] = pair[:, :HEAD_DIM]
                vwin[at : at + CHUNK, :] = pair[:, HEAD_DIM:]
        columns = base + skipped * CHUNK + lax.broadcasted_iota(jnp.int32, (CHUNK, width), 1)
        allowed = (columns >= starts) & (columns <= tokens)
        bias = jnp.where(allowed, 0.0, MASK_FILL).astype(F32)[None]
        dwin[:, :width] = jnp.zeros((2 * HEAD_DIM, width), F32)

        def block(number, carry):
            lanes = pl.multiple_of(number * (HEADS_STEP * HEAD_DIM), HEADS_STEP * HEAD_DIM)
            span = pl.ds(lanes, HEADS_STEP * HEAD_DIM)
            other = pl.ds(WIDE + lanes, HEADS_STEP * HEAD_DIM)
            q_all = qdo_ref[:, span]
            do_all = qdo_ref[:, other]

            def stack(block_all):
                return jnp.concatenate(
                    [block_all[:, h * HEAD_DIM : (h + 1) * HEAD_DIM] for h in range(HEADS_STEP)], 0
                )

            def unstack(rows):
                return jnp.concatenate(
                    [rows[h * CHUNK : (h + 1) * CHUNK] for h in range(HEADS_STEP)], 1
                )

            q = stack(q_all)
            do = stack(do_all)
            keys = kwin[:width, :]
            values = vwin[:width, :]
            scores = (dot_t(q, keys) * SCALE_LOG2).reshape(HEADS_STEP, CHUNK, width) + bias
            scores = scores.reshape(ROWS_STEP, width)
            highest = jnp.max(scores, axis=-1, keepdims=True)
            powers = jnp.exp2(scores - highest)
            total = jnp.sum(powers, axis=-1, keepdims=True)
            probabilities = powers * (1.0 / total)
            weights = probabilities.astype(BF16)
            attended = dot(weights, values).astype(BF16)
            delta = jnp.sum(do.astype(F32) * attended.astype(F32), axis=-1, keepdims=True)
            slopes = (probabilities * (dot_t(do, values) - delta)).astype(BF16)
            odq_ref[:, span] = unstack(attended)
            odq_ref[:, other] = unstack((dot(slopes, keys) * SCALE).astype(BF16))
            dwin[:HEAD_DIM, :width] += dot(q.astype(F32).T.astype(BF16), slopes)
            dwin[HEAD_DIM:, :width] += dot(do.astype(F32).T.astype(BF16), weights)
            return carry

        lax.fori_loop(0, GROUP // HEADS_STEP, block, 0)
        back = dwin[:, :width].T
        for t in range(skipped, REACH + 1):
            at = (t - skipped) * CHUNK
            acc[t % RING, unit(t)] += back[at : at + CHUNK, :]

    for index, chunks in enumerate(CLASSES):
        fits = needed <= chunks
        if index == 0:
            fits = needed > CLASSES[1]
        elif index + 1 < len(CLASSES):
            fits = fits & (needed > CLASSES[index + 1])
        pl.when(fits)(functools.partial(run, chunks))

    @pl.when(step == ROW - 1)
    def _():
        for slot in range(RING):
            whole = acc[slot]
            keys_part = (whole[:, :, :HEAD_DIM] * SCALE).astype(BF16)
            values_part = whole[:, :, HEAD_DIM:].astype(BF16)
            if slot == RING // 2:
                dkv_refs[slot][...] = keys_part
                dv4_ref[...] = values_part
            else:
                dkv_refs[slot][:, :, :HEAD_DIM] = keys_part
                dkv_refs[slot][:, :, HEAD_DIM:] = values_part


def attention(place, lengths, qdo, slots, v4):
    rows = pl.BlockSpec((CHUNK, 2 * WIDE), lambda i, *_: (i, 0))

    def whole(shape):
        return pl.BlockSpec(shape, lambda i, *_: (0, 0, 0))

    pair = (UNITS, CHUNK, 2 * HEAD_DIM)
    single = (UNITS, CHUNK, HEAD_DIM)
    shapes = [single if slot == RING // 2 else pair for slot in range(RING)] + [single]
    kv_specs = [whole(shape) for shape in shapes]
    big = jax.ShapeDtypeStruct((ROW * CHUNK, 2 * WIDE), BF16)
    return pl.pallas_call(
        attention_kernel,
        out_shape=[big] + [jax.ShapeDtypeStruct(shape, BF16) for shape in shapes],
        grid_spec=pltpu.PrefetchScalarGridSpec(
            num_scalar_prefetch=2,
            grid=(ROW,),
            in_specs=[rows] + kv_specs,
            out_specs=[rows] + kv_specs,
            scratch_shapes=[
                pltpu.VMEM((WINDOW, HEAD_DIM), BF16),
                pltpu.VMEM((WINDOW, HEAD_DIM), BF16),
                pltpu.VMEM((2 * HEAD_DIM, WINDOW), F32),
                pltpu.VMEM((RING, UNITS, CHUNK, 2 * HEAD_DIM), F32),
            ],
        ),
        compiler_params=pltpu.CompilerParams(vmem_limit_bytes=56 * 1024 * 1024),
    )(place, lengths, qdo, *slots, v4)


def around(value, step):
    return lax.ppermute(value, "z", [(i, (i + step) % RING) for i in range(RING)])


def exchanged(value):
    return lax.all_to_all(value, HEAD_AXES, split_axis=0, concat_axis=0, tiled=True)


def split_kernel(a_ref, b_ref, out_ref):
    width = out_ref.shape[2] // 2
    for g in range(out_ref.shape[0]):
        out_ref[g, :, :width] = a_ref[:, g * width : (g + 1) * width]
        out_ref[g, :, width:] = b_ref[:, g * width : (g + 1) * width]


def split_heads(a, b, steps):
    rows, width = a.shape[0], a.shape[1] // KV_HEADS
    count = KV_HEADS // steps
    part = pl.BlockSpec((rows, count * width), lambda g: (0, g))
    return pl.pallas_call(
        split_kernel,
        out_shape=jax.ShapeDtypeStruct((KV_HEADS, rows, 2 * width), a.dtype),
        grid=(steps,),
        in_specs=[part, part],
        out_specs=pl.BlockSpec((count, rows, 2 * width), lambda g: (g, 0, 0)),
    )(a, b)


def merge_kernel(in_ref, a_ref, b_ref):
    width = in_ref.shape[2] // 2
    for g in range(in_ref.shape[0]):
        a_ref[:, g * width : (g + 1) * width] = in_ref[g, :, :width]
        b_ref[:, g * width : (g + 1) * width] = in_ref[g, :, width:]


def merge_heads(value, steps):
    groups, rows, width = value.shape[0], value.shape[1], value.shape[2] // 2
    count = groups // steps
    part = pl.BlockSpec((rows, count * width), lambda g: (0, g))
    whole = jax.ShapeDtypeStruct((rows, groups * width), value.dtype)
    return pl.pallas_call(
        merge_kernel,
        out_shape=[whole, whole],
        grid=(steps,),
        in_specs=[pl.BlockSpec((count, rows, 2 * width), lambda g: (g, 0, 0))],
        out_specs=[part, part],
    )(value)


def added(a, b):
    return (a.astype(F32) + b.astype(F32)).astype(BF16)


def body(queries, key_vectors, value_vectors, output_cotangent, doc_lengths):
    local = key_vectors.shape[0]
    tokens = KV_HEADS * local
    own = exchanged(split_heads(key_vectors, value_vectors, 1)).reshape(tokens, 2 * HEAD_DIM)
    qdo = exchanged(split_heads(queries, output_cotangent, 2)).reshape(tokens, 2 * WIDE)
    half = 2 * CHUNK
    earlier = lax.ppermute(own[half:], "y", [(i, i + 1) for i in range(ROW - 1)])
    units = jnp.concatenate([earlier, own], axis=0)
    middle = RING // 2
    slots = [None] * RING
    slots[0] = units
    up = down = units
    for step in range(1, middle):
        up, down = around(up, 1), around(down, -1)
        slots[RING - step], slots[step] = up, down
    slots[middle] = around(up[:, :HEAD_DIM], 1)
    last_values = around(down[:, HEAD_DIM:], -1)
    place = jnp.stack([lax.axis_index("y"), lax.axis_index("z")]).astype(jnp.int32)
    slots = [s.reshape(UNITS, CHUNK, -1) for s in slots]
    results = attention(
        place, doc_lengths, qdo, slots, last_values.reshape(UNITS, CHUNK, HEAD_DIM)
    )
    odq = exchanged(results[0].reshape(KV_HEADS, local, 2 * WIDE))
    parts = [r.reshape(UNITS * CHUNK, -1) for r in results[1:]]
    up = around(parts[middle], 1)
    down = around(parts[RING], -1)
    up = jnp.concatenate(
        [added(parts[middle - 1][:, :HEAD_DIM], up), parts[middle - 1][:, HEAD_DIM:]], 1
    )
    down = jnp.concatenate(
        [parts[middle + 1][:, :HEAD_DIM], added(parts[middle + 1][:, HEAD_DIM:], down)], 1
    )
    for step in range(middle - 2, 0, -1):
        up = added(parts[step], around(up, 1))
        down = added(parts[RING - step], around(down, -1))
    mine = parts[0].astype(F32) + around(up, 1).astype(F32) + around(down, -1).astype(F32)
    returned = lax.ppermute(mine[:half].astype(BF16), "y", [(i, i - 1) for i in range(1, ROW)])
    total = jnp.concatenate([mine[half : 2 * half], mine[2 * half :] + returned.astype(F32)], 0)
    total = total.astype(BF16).reshape(KV_HEADS, local, 2 * HEAD_DIM)
    total, odq = lax.optimization_barrier((total, odq))
    attended, query_slope = merge_heads(odq, 2)
    key_slope, value_slope = merge_heads(exchanged(total), 1)
    return attended, query_slope, key_slope, value_slope


def solution(mesh):
    split = Mesh(mesh.devices.reshape(ROW, ROW, RING, 2), ("y", "x", "z", "core"))
    rows = P(("y", "x", "z", "core"), None)
    return jax.shard_map(
        body,
        mesh=split,
        in_specs=(rows, rows, rows, rows, P()),
        out_specs=(rows, rows, rows, rows),
        check_vma=False,
    )
```

```python
import functools
import math

import jax
import jax.numpy as jnp
from jax import lax
from jax.experimental import pallas as pl
from jax.experimental.pallas import tpu as pltpu
from jax.sharding import Mesh, PartitionSpec as P

HEAD_DIM = 128
KV_HEADS = 8
GROUP = 16
NDOC = 16
CHUNK = 64
RING = 8
ROW = 4
UNITS = ROW + 2
REACH = 16
WINDOW = (REACH + 1) * CHUNK
CLASSES = (17, 13, 11, 9, 7, 5, 3)
HEADS_STEP = 16
ROWS_STEP = HEADS_STEP * CHUNK
MASK_FILL = -1e30
SCALE = 1.0 / math.sqrt(HEAD_DIM)
SCALE_LOG2 = SCALE * math.log2(math.e)
BF16 = jnp.bfloat16
F32 = jnp.float32
HEAD_AXES = ("x", "core")
WIDE = GROUP * HEAD_DIM


def dot_t(a, b):
    return lax.dot_general(a, b, (((1,), (1,)), ((), ())), preferred_element_type=F32)


def dot(a, b):
    return jnp.dot(a, b, preferred_element_type=F32)


def attention_kernel(place, lengths, qdo_ref, *refs):
    kv_refs = refs[:RING]
    v4_ref = refs[RING]
    odq_ref = refs[RING + 1]
    dkv_refs = refs[RING + 2 : 2 * RING + 2]
    dv4_ref = refs[2 * RING + 2]
    kwin, vwin, dwin, acc = refs[2 * RING + 3 :]
    step = pl.program_id(0)
    z = place[1]
    first = ((place[0] * ROW + step) * RING + z) * CHUNK
    base = first - REACH * CHUNK

    @pl.when(step == 0)
    def _():
        acc[...] = jnp.zeros_like(acc)

    def unit(t):
        return step + t // RING + (z + t % RING >= RING).astype(jnp.int32)

    tokens = first + lax.broadcasted_iota(jnp.int32, (CHUNK, 1), 0)
    starts = jnp.zeros((CHUNK, 1), jnp.int32)
    ending = jnp.int32(0)
    earliest = jnp.int32(0)
    for d in range(NDOC):
        ending = ending + lengths[d]
        starts = jnp.where(tokens >= ending, ending, starts)
        earliest = jnp.where(first >= ending, ending, earliest)
    needed = REACH + 1 - (earliest - base) // CHUNK

    def run(chunks):
        skipped = REACH + 1 - chunks
        width = chunks * CHUNK
        for t in range(skipped, REACH + 1):
            at = (t - skipped) * CHUNK
            slot = t % RING
            if slot == RING // 2:
                kwin[at : at + CHUNK, :] = kv_refs[slot][unit(t)]
                vwin[at : at + CHUNK, :] = v4_ref[unit(t)]
            else:
                pair = kv_refs[slot][unit(t)]
                kwin[at : at + CHUNK, :] = pair[:, :HEAD_DIM]
                vwin[at : at + CHUNK, :] = pair[:, HEAD_DIM:]
        columns = base + skipped * CHUNK + lax.broadcasted_iota(jnp.int32, (CHUNK, width), 1)
        allowed = (columns >= starts) & (columns <= tokens)
        bias = jnp.where(allowed, 0.0, MASK_FILL).astype(F32)[None]
        dwin[:, :width] = jnp.zeros((2 * HEAD_DIM, width), F32)

        def block(number, carry):
            lanes = pl.multiple_of(number * (HEADS_STEP * HEAD_DIM), HEADS_STEP * HEAD_DIM)
            span = pl.ds(lanes, HEADS_STEP * HEAD_DIM)
            other = pl.ds(WIDE + lanes, HEADS_STEP * HEAD_DIM)
            q_all = qdo_ref[:, span]
            do_all = qdo_ref[:, other]

            def stack(block_all):
                return jnp.concatenate(
                    [block_all[:, h * HEAD_DIM : (h + 1) * HEAD_DIM] for h in range(HEADS_STEP)], 0
                )

            def unstack(rows):
                return jnp.concatenate(
                    [rows[h * CHUNK : (h + 1) * CHUNK] for h in range(HEADS_STEP)], 1
                )

            q = stack(q_all)
            do = stack(do_all)
            keys = kwin[:width, :]
            values = vwin[:width, :]
            scores = (dot_t(q, keys) * SCALE_LOG2).reshape(HEADS_STEP, CHUNK, width) + bias
            scores = scores.reshape(ROWS_STEP, width)
            highest = jnp.max(scores, axis=-1, keepdims=True)
            powers = jnp.exp2(scores - highest)
            total = jnp.sum(powers, axis=-1, keepdims=True)
            probabilities = powers * (1.0 / total)
            weights = probabilities.astype(BF16)
            attended = dot(weights, values).astype(BF16)
            delta = jnp.sum(do.astype(F32) * attended.astype(F32), axis=-1, keepdims=True)
            slopes = (probabilities * (dot_t(do, values) - delta)).astype(BF16)
            odq_ref[:, span] = unstack(attended)
            odq_ref[:, other] = unstack((dot(slopes, keys) * SCALE).astype(BF16))
            dwin[:HEAD_DIM, :width] += dot(q.astype(F32).T.astype(BF16), slopes)
            dwin[HEAD_DIM:, :width] += dot(do.astype(F32).T.astype(BF16), weights)
            return carry

        lax.fori_loop(0, GROUP // HEADS_STEP, block, 0)
        back = dwin[:, :width].T
        for t in range(skipped, REACH + 1):
            at = (t - skipped) * CHUNK
            acc[t % RING, unit(t)] += back[at : at + CHUNK, :]

    for index, chunks in enumerate(CLASSES):
        fits = needed <= chunks
        if index == 0:
            fits = needed > CLASSES[1]
        elif index + 1 < len(CLASSES):
            fits = fits & (needed > CLASSES[index + 1])
        pl.when(fits)(functools.partial(run, chunks))

    @pl.when(step == ROW - 1)
    def _():
        for slot in range(RING):
            whole = acc[slot]
            keys_part = (whole[:, :, :HEAD_DIM] * SCALE).astype(BF16)
            values_part = whole[:, :, HEAD_DIM:].astype(BF16)
            if slot == RING // 2:
                dkv_refs[slot][...] = keys_part
                dv4_ref[...] = values_part
            else:
                dkv_refs[slot][:, :, :HEAD_DIM] = keys_part
                dkv_refs[slot][:, :, HEAD_DIM:] = values_part


def attention(place, lengths, qdo, slots, v4):
    rows = pl.BlockSpec((CHUNK, 2 * WIDE), lambda i, *_: (i, 0))

    def whole(shape):
        return pl.BlockSpec(shape, lambda i, *_: (0, 0, 0))

    pair = (UNITS, CHUNK, 2 * HEAD_DIM)
    single = (UNITS, CHUNK, HEAD_DIM)
    shapes = [single if slot == RING // 2 else pair for slot in range(RING)] + [single]
    kv_specs = [whole(shape) for shape in shapes]
    big = jax.ShapeDtypeStruct((ROW * CHUNK, 2 * WIDE), BF16)
    return pl.pallas_call(
        attention_kernel,
        out_shape=[big] + [jax.ShapeDtypeStruct(shape, BF16) for shape in shapes],
        grid_spec=pltpu.PrefetchScalarGridSpec(
            num_scalar_prefetch=2,
            grid=(ROW,),
            in_specs=[rows] + kv_specs,
            out_specs=[rows] + kv_specs,
            scratch_shapes=[
                pltpu.VMEM((WINDOW, HEAD_DIM), BF16),
                pltpu.VMEM((WINDOW, HEAD_DIM), BF16),
                pltpu.VMEM((2 * HEAD_DIM, WINDOW), F32),
                pltpu.VMEM((RING, UNITS, CHUNK, 2 * HEAD_DIM), F32),
            ],
        ),
        compiler_params=pltpu.CompilerParams(vmem_limit_bytes=56 * 1024 * 1024),
    )(place, lengths, qdo, *slots, v4)


def around(value, step):
    return lax.ppermute(value, "z", [(i, (i + step) % RING) for i in range(RING)])


def exchanged(value):
    return lax.all_to_all(value, HEAD_AXES, split_axis=0, concat_axis=0, tiled=True)


def split_kernel(a_ref, b_ref, out_ref):
    width = out_ref.shape[2] // 2
    for g in range(out_ref.shape[0]):
        out_ref[g, :, :width] = a_ref[:, g * width : (g + 1) * width]
        out_ref[g, :, width:] = b_ref[:, g * width : (g + 1) * width]


def split_heads(a, b, steps):
    rows, width = a.shape[0], a.shape[1] // KV_HEADS
    count = KV_HEADS // steps
    part = pl.BlockSpec((rows, count * width), lambda g: (0, g))
    return pl.pallas_call(
        split_kernel,
        out_shape=jax.ShapeDtypeStruct((KV_HEADS, rows, 2 * width), a.dtype),
        grid=(steps,),
        in_specs=[part, part],
        out_specs=pl.BlockSpec((count, rows, 2 * width), lambda g: (g, 0, 0)),
    )(a, b)


def merge_kernel(in_ref, a_ref, b_ref):
    width = in_ref.shape[2] // 2
    for g in range(in_ref.shape[0]):
        a_ref[:, g * width : (g + 1) * width] = in_ref[g, :, :width]
        b_ref[:, g * width : (g + 1) * width] = in_ref[g, :, width:]


def merge_heads(value, steps):
    groups, rows, width = value.shape[0], value.shape[1], value.shape[2] // 2
    count = groups // steps
    part = pl.BlockSpec((rows, count * width), lambda g: (0, g))
    whole = jax.ShapeDtypeStruct((rows, groups * width), value.dtype)
    return pl.pallas_call(
        merge_kernel,
        out_shape=[whole, whole],
        grid=(steps,),
        in_specs=[pl.BlockSpec((count, rows, 2 * width), lambda g: (g, 0, 0))],
        out_specs=[part, part],
    )(value)


def added(a, b):
    return (a.astype(F32) + b.astype(F32)).astype(BF16)


def body(queries, key_vectors, value_vectors, output_cotangent, doc_lengths):
    local = key_vectors.shape[0]
    tokens = KV_HEADS * local
    own = exchanged(split_heads(key_vectors, value_vectors, 1)).reshape(tokens, 2 * HEAD_DIM)
    qdo = exchanged(split_heads(queries, output_cotangent, 2)).reshape(tokens, 2 * WIDE)
    half = 2 * CHUNK
    earlier = lax.ppermute(own[half:], "y", [(i, i + 1) for i in range(ROW - 1)])
    units = jnp.concatenate([earlier, own], axis=0)
    middle = RING // 2
    slots = [None] * RING
    slots[0] = units
    up = down = units
    for step in range(1, middle):
        up, down = around(up, 1), around(down, -1)
        slots[RING - step], slots[step] = up, down
    up, down, qdo = lax.optimization_barrier((up, down, qdo))
    slots[middle] = around(up[:, :HEAD_DIM], 1)
    last_values = around(down[:, HEAD_DIM:], -1)
    place = jnp.stack([lax.axis_index("y"), lax.axis_index("z")]).astype(jnp.int32)
    slots = [s.reshape(UNITS, CHUNK, -1) for s in slots]
    results = attention(
        place, doc_lengths, qdo, slots, last_values.reshape(UNITS, CHUNK, HEAD_DIM)
    )
    odq = exchanged(results[0].reshape(KV_HEADS, local, 2 * WIDE))
    parts = [r.reshape(UNITS * CHUNK, -1) for r in results[1:]]
    up = around(parts[middle], 1)
    down = around(parts[RING], -1)
    up = jnp.concatenate(
        [added(parts[middle - 1][:, :HEAD_DIM], up), parts[middle - 1][:, HEAD_DIM:]], 1
    )
    down = jnp.concatenate(
        [parts[middle + 1][:, :HEAD_DIM], added(parts[middle + 1][:, HEAD_DIM:], down)], 1
    )
    for step in range(middle - 2, 0, -1):
        up = added(parts[step], around(up, 1))
        down = added(parts[RING - step], around(down, -1))
    mine = parts[0].astype(F32) + around(up, 1).astype(F32) + around(down, -1).astype(F32)
    returned = lax.ppermute(mine[:half].astype(BF16), "y", [(i, i - 1) for i in range(1, ROW)])
    total = jnp.concatenate([mine[half : 2 * half], mine[2 * half :] + returned.astype(F32)], 0)
    total = total.astype(BF16).reshape(KV_HEADS, local, 2 * HEAD_DIM)
    total, odq = lax.optimization_barrier((total, odq))
    attended, query_slope = merge_heads(odq, 2)
    key_slope, value_slope = merge_heads(exchanged(total), 1)
    return attended, query_slope, key_slope, value_slope


def solution(mesh):
    split = Mesh(mesh.devices.reshape(ROW, ROW, RING, 2), ("y", "x", "z", "core"))
    rows = P(("y", "x", "z", "core"), None)
    return jax.shard_map(
        body,
        mesh=split,
        in_specs=(rows, rows, rows, rows, P()),
        out_specs=(rows, rows, rows, rows),
        check_vma=False,
    )
```

```python
import functools
import math

import jax
import jax.numpy as jnp
from jax import lax
from jax.experimental import pallas as pl
from jax.experimental.pallas import tpu as pltpu
from jax.sharding import Mesh, PartitionSpec as P

HEAD_DIM = 128
KV_HEADS = 8
GROUP = 16
NDOC = 16
CHUNK = 64
RING = 8
ROW = 4
UNITS = ROW + 2
REACH = 16
WINDOW = (REACH + 1) * CHUNK
CLASSES = (17, 13, 11, 9, 7, 5, 3)
HEADS_STEP = 16
ROWS_STEP = HEADS_STEP * CHUNK
MASK_FILL = -1e30
SCALE = 1.0 / math.sqrt(HEAD_DIM)
SCALE_LOG2 = SCALE * math.log2(math.e)
BF16 = jnp.bfloat16
F32 = jnp.float32
HEAD_AXES = ("x", "core")
WIDE = GROUP * HEAD_DIM


def dot_t(a, b):
    return lax.dot_general(a, b, (((1,), (1,)), ((), ())), preferred_element_type=F32)


def dot(a, b):
    return jnp.dot(a, b, preferred_element_type=F32)


def attention_kernel(place, lengths, qdo_ref, *refs):
    kv_refs = refs[:RING]
    v4_ref = refs[RING]
    odq_ref = refs[RING + 1]
    dkv_refs = refs[RING + 2 : 2 * RING + 2]
    kwin, vwin, dwin, acc = refs[2 * RING + 2 :]
    step = pl.program_id(0)
    z = place[1]
    first = ((place[0] * ROW + step) * RING + z) * CHUNK
    base = first - REACH * CHUNK

    @pl.when(step == 0)
    def _():
        acc[...] = jnp.zeros_like(acc)

    def unit(t):
        return step + t // RING + (z + t % RING >= RING).astype(jnp.int32)

    tokens = first + lax.broadcasted_iota(jnp.int32, (CHUNK, 1), 0)
    starts = jnp.zeros((CHUNK, 1), jnp.int32)
    ending = jnp.int32(0)
    earliest = jnp.int32(0)
    for d in range(NDOC):
        ending = ending + lengths[d]
        starts = jnp.where(tokens >= ending, ending, starts)
        earliest = jnp.where(first >= ending, ending, earliest)
    needed = REACH + 1 - (earliest - base) // CHUNK

    def run(chunks):
        skipped = REACH + 1 - chunks
        width = chunks * CHUNK
        for t in range(skipped, REACH + 1):
            at = (t - skipped) * CHUNK
            slot = t % RING
            if slot == RING // 2:
                kwin[at : at + CHUNK, :] = kv_refs[slot][unit(t)]
                vwin[at : at + CHUNK, :] = v4_ref[unit(t)]
            else:
                pair = kv_refs[slot][unit(t)]
                kwin[at : at + CHUNK, :] = pair[:, :HEAD_DIM]
                vwin[at : at + CHUNK, :] = pair[:, HEAD_DIM:]
        columns = base + skipped * CHUNK + lax.broadcasted_iota(jnp.int32, (CHUNK, width), 1)
        allowed = (columns >= starts) & (columns <= tokens)
        bias = jnp.where(allowed, 0.0, MASK_FILL).astype(F32)[None]
        dwin[:, :width] = jnp.zeros((2 * HEAD_DIM, width), F32)

        def block(number, carry):
            lanes = pl.multiple_of(number * (HEADS_STEP * HEAD_DIM), HEADS_STEP * HEAD_DIM)
            span = pl.ds(lanes, HEADS_STEP * HEAD_DIM)
            other = pl.ds(WIDE + lanes, HEADS_STEP * HEAD_DIM)
            q_all = qdo_ref[:, span]
            do_all = qdo_ref[:, other]

            def stack(block_all):
                return jnp.concatenate(
                    [block_all[:, h * HEAD_DIM : (h + 1) * HEAD_DIM] for h in range(HEADS_STEP)], 0
                )

            def unstack(rows):
                return jnp.concatenate(
                    [rows[h * CHUNK : (h + 1) * CHUNK] for h in range(HEADS_STEP)], 1
                )

            q = stack(q_all)
            do = stack(do_all)
            keys = kwin[:width, :]
            values = vwin[:width, :]
            scores = (dot_t(q, keys) * SCALE_LOG2).reshape(HEADS_STEP, CHUNK, width) + bias
            scores = scores.reshape(ROWS_STEP, width)
            highest = jnp.max(scores, axis=-1, keepdims=True)
            powers = jnp.exp2(scores - highest)
            total = jnp.sum(powers, axis=-1, keepdims=True)
            probabilities = powers * (1.0 / total)
            weights = probabilities.astype(BF16)
            attended = dot(weights, values).astype(BF16)
            delta = jnp.sum(do.astype(F32) * attended.astype(F32), axis=-1, keepdims=True)
            slopes = (probabilities * (dot_t(do, values) - delta)).astype(BF16)
            odq_ref[:, span] = unstack(attended)
            odq_ref[:, other] = unstack((dot(slopes, keys) * SCALE).astype(BF16))
            dwin[:HEAD_DIM, :width] += dot(q.astype(F32).T.astype(BF16), slopes)
            dwin[HEAD_DIM:, :width] += dot(do.astype(F32).T.astype(BF16), weights)
            return carry

        lax.fori_loop(0, GROUP // HEADS_STEP, block, 0)
        back = dwin[:, :width].T
        for t in range(skipped, REACH + 1):
            at = (t - skipped) * CHUNK
            acc[t % RING, unit(t)] += back[at : at + CHUNK, :]

    for index, chunks in enumerate(CLASSES):
        fits = needed <= chunks
        if index == 0:
            fits = needed > CLASSES[1]
        elif index + 1 < len(CLASSES):
            fits = fits & (needed > CLASSES[index + 1])
        pl.when(fits)(functools.partial(run, chunks))

    @pl.when(step == ROW - 1)
    def _():
        for slot in range(RING):
            whole = acc[slot]
            dkv_refs[slot][:, :, :HEAD_DIM] = (whole[:, :, :HEAD_DIM] * SCALE).astype(BF16)
            dkv_refs[slot][:, :, HEAD_DIM:] = whole[:, :, HEAD_DIM:].astype(BF16)


def attention(place, lengths, qdo, slots, v4):
    rows = pl.BlockSpec((CHUNK, 2 * WIDE), lambda i, *_: (i, 0))

    def whole(shape):
        return pl.BlockSpec(shape, lambda i, *_: (0, 0, 0))

    pair = (UNITS, CHUNK, 2 * HEAD_DIM)
    single = (UNITS, CHUNK, HEAD_DIM)
    shapes = [single if slot == RING // 2 else pair for slot in range(RING)] + [single]
    kv_specs = [whole(shape) for shape in shapes]
    big = jax.ShapeDtypeStruct((ROW * CHUNK, 2 * WIDE), BF16)
    return pl.pallas_call(
        attention_kernel,
        out_shape=[big] + [jax.ShapeDtypeStruct(pair, BF16)] * RING,
        grid_spec=pltpu.PrefetchScalarGridSpec(
            num_scalar_prefetch=2,
            grid=(ROW,),
            in_specs=[rows] + kv_specs,
            out_specs=[rows] + [whole(pair)] * RING,
            scratch_shapes=[
                pltpu.VMEM((WINDOW, HEAD_DIM), BF16),
                pltpu.VMEM((WINDOW, HEAD_DIM), BF16),
                pltpu.VMEM((2 * HEAD_DIM, WINDOW), F32),
                pltpu.VMEM((RING, UNITS, CHUNK, 2 * HEAD_DIM), F32),
            ],
        ),
        compiler_params=pltpu.CompilerParams(vmem_limit_bytes=56 * 1024 * 1024),
    )(place, lengths, qdo, *slots, v4)


def around(value, step):
    return lax.ppermute(value, "z", [(i, (i + step) % RING) for i in range(RING)])


def exchanged(value):
    return lax.all_to_all(value, HEAD_AXES, split_axis=0, concat_axis=0, tiled=True)


def split_kernel(a_ref, b_ref, out_ref):
    width = out_ref.shape[2] // 2
    for g in range(out_ref.shape[0]):
        out_ref[g, :, :width] = a_ref[:, g * width : (g + 1) * width]
        out_ref[g, :, width:] = b_ref[:, g * width : (g + 1) * width]


def split_heads(a, b, steps):
    rows, width = a.shape[0], a.shape[1] // KV_HEADS
    count = KV_HEADS // steps
    part = pl.BlockSpec((rows, count * width), lambda g: (0, g))
    return pl.pallas_call(
        split_kernel,
        out_shape=jax.ShapeDtypeStruct((KV_HEADS, rows, 2 * width), a.dtype),
        grid=(steps,),
        in_specs=[part, part],
        out_specs=pl.BlockSpec((count, rows, 2 * width), lambda g: (g, 0, 0)),
    )(a, b)


def merge_kernel(in_ref, a_ref, b_ref):
    width = in_ref.shape[2] // 2
    for g in range(in_ref.shape[0]):
        a_ref[:, g * width : (g + 1) * width] = in_ref[g, :, :width]
        b_ref[:, g * width : (g + 1) * width] = in_ref[g, :, width:]


def merge_heads(value, steps):
    groups, rows, width = value.shape[0], value.shape[1], value.shape[2] // 2
    count = groups // steps
    part = pl.BlockSpec((rows, count * width), lambda g: (0, g))
    whole = jax.ShapeDtypeStruct((rows, groups * width), value.dtype)
    return pl.pallas_call(
        merge_kernel,
        out_shape=[whole, whole],
        grid=(steps,),
        in_specs=[pl.BlockSpec((count, rows, 2 * width), lambda g: (g, 0, 0))],
        out_specs=[part, part],
    )(value)


def added(a, b):
    return (a.astype(F32) + b.astype(F32)).astype(BF16)


def body(queries, key_vectors, value_vectors, output_cotangent, doc_lengths):
    local = key_vectors.shape[0]
    tokens = KV_HEADS * local
    own = exchanged(split_heads(key_vectors, value_vectors, 1)).reshape(tokens, 2 * HEAD_DIM)
    qdo = exchanged(split_heads(queries, output_cotangent, 2)).reshape(tokens, 2 * WIDE)
    half = 2 * CHUNK
    earlier = lax.ppermute(own[half:], "y", [(i, i + 1) for i in range(ROW - 1)])
    units = jnp.concatenate([earlier, own], axis=0)
    middle = RING // 2
    slots = [None] * RING
    slots[0] = units
    up = down = units
    for step in range(1, middle):
        up, down = around(up, 1), around(down, -1)
        slots[RING - step], slots[step] = up, down
    up, down, qdo = lax.optimization_barrier((up, down, qdo))
    slots[middle] = around(up[:, :HEAD_DIM], 1)
    last_values = around(down[:, HEAD_DIM:], -1)
    place = jnp.stack([lax.axis_index("y"), lax.axis_index("z")]).astype(jnp.int32)
    slots = [s.reshape(UNITS, CHUNK, -1) for s in slots]
    results = attention(
        place, doc_lengths, qdo, slots, last_values.reshape(UNITS, CHUNK, HEAD_DIM)
    )
    odq = exchanged(results[0].reshape(KV_HEADS, local, 2 * WIDE))
    parts = [r.reshape(UNITS * CHUNK, -1) for r in results[1:]]
    up = added(parts[middle - 1], around(parts[middle], 1))
    down = parts[middle + 1]
    for step in range(middle - 2, 0, -1):
        up = added(parts[step], around(up, 1))
        down = added(parts[RING - step], around(down, -1))
    mine = parts[0].astype(F32) + around(up, 1).astype(F32) + around(down, -1).astype(F32)
    returned = lax.ppermute(mine[:half].astype(BF16), "y", [(i, i - 1) for i in range(1, ROW)])
    total = jnp.concatenate([mine[half : 2 * half], mine[2 * half :] + returned.astype(F32)], 0)
    total = total.astype(BF16).reshape(KV_HEADS, local, 2 * HEAD_DIM)
    total, odq = lax.optimization_barrier((total, odq))
    attended, query_slope = merge_heads(odq, 2)
    slopes = jnp.swapaxes(exchanged(total), 0, 1)
    key_slope = slopes[:, :, :HEAD_DIM].reshape(local, KV_HEADS * HEAD_DIM)
    value_slope = slopes[:, :, HEAD_DIM:].reshape(local, KV_HEADS * HEAD_DIM)
    return attended, query_slope, key_slope, value_slope


def solution(mesh):
    split = Mesh(mesh.devices.reshape(ROW, ROW, RING, 2), ("y", "x", "z", "core"))
    rows = P(("y", "x", "z", "core"), None)
    return jax.shard_map(
        body,
        mesh=split,
        in_specs=(rows, rows, rows, rows, P()),
        out_specs=(rows, rows, rows, rows),
        check_vma=False,
    )
```

```python
import functools
import math

import jax
import jax.numpy as jnp
from jax import lax
from jax.experimental import pallas as pl
from jax.experimental.pallas import tpu as pltpu
from jax.sharding import Mesh, PartitionSpec as P

HEAD_DIM = 128
KV_HEADS = 8
GROUP = 16
NDOC = 16
CHUNK = 64
RING = 8
ROW = 4
UNITS = ROW + 2
REACH = 16
WINDOW = (REACH + 1) * CHUNK
CLASSES = (17, 14, 12, 10, 8, 6, 4)
HEADS_STEP = 16
ROWS_STEP = HEADS_STEP * CHUNK
MASK_FILL = -1e30
SCALE = 1.0 / math.sqrt(HEAD_DIM)
SCALE_LOG2 = SCALE * math.log2(math.e)
BF16 = jnp.bfloat16
F32 = jnp.float32
HEAD_AXES = ("x", "core")
WIDE = GROUP * HEAD_DIM


def dot_t(a, b):
    return lax.dot_general(a, b, (((1,), (1,)), ((), ())), preferred_element_type=F32)


def dot(a, b):
    return jnp.dot(a, b, preferred_element_type=F32)


def attention_kernel(place, lengths, qdo_ref, *refs):
    kv_refs = refs[:RING]
    v4_ref = refs[RING]
    odq_ref = refs[RING + 1]
    dkv_refs = refs[RING + 2 : 2 * RING + 2]
    kwin, vwin, dwin, acc = refs[2 * RING + 2 :]
    step = pl.program_id(0)
    z = place[1]
    first = ((place[0] * ROW + step) * RING + z) * CHUNK
    base = first - REACH * CHUNK

    @pl.when(step == 0)
    def _():
        acc[...] = jnp.zeros_like(acc)

    def unit(t):
        return step + t // RING + (z + t % RING >= RING).astype(jnp.int32)

    tokens = first + lax.broadcasted_iota(jnp.int32, (CHUNK, 1), 0)
    starts = jnp.zeros((CHUNK, 1), jnp.int32)
    ending = jnp.int32(0)
    earliest = jnp.int32(0)
    for d in range(NDOC):
        ending = ending + lengths[d]
        starts = jnp.where(tokens >= ending, ending, starts)
        earliest = jnp.where(first >= ending, ending, earliest)
    needed = REACH + 1 - (earliest - base) // CHUNK

    def run(chunks):
        skipped = REACH + 1 - chunks
        width = chunks * CHUNK
        for t in range(skipped, REACH + 1):
            at = (t - skipped) * CHUNK
            slot = t % RING
            if slot == RING // 2:
                kwin[at : at + CHUNK, :] = kv_refs[slot][unit(t)]
                vwin[at : at + CHUNK, :] = v4_ref[unit(t)]
            else:
                pair = kv_refs[slot][unit(t)]
                kwin[at : at + CHUNK, :] = pair[:, :HEAD_DIM]
                vwin[at : at + CHUNK, :] = pair[:, HEAD_DIM:]
        columns = base + skipped * CHUNK + lax.broadcasted_iota(jnp.int32, (CHUNK, width), 1)
        allowed = (columns >= starts) & (columns <= tokens)
        bias = jnp.where(allowed, 0.0, MASK_FILL).astype(F32)[None]
        def block(number, carry):
            lanes = pl.multiple_of(number * (HEADS_STEP * HEAD_DIM), HEADS_STEP * HEAD_DIM)
            span = pl.ds(lanes, HEADS_STEP * HEAD_DIM)
            other = pl.ds(WIDE + lanes, HEADS_STEP * HEAD_DIM)
            q_all = qdo_ref[:, span]
            do_all = qdo_ref[:, other]

            def stack(block_all):
                return jnp.concatenate(
                    [block_all[:, h * HEAD_DIM : (h + 1) * HEAD_DIM] for h in range(HEADS_STEP)], 0
                )

            def unstack(rows):
                return jnp.concatenate(
                    [rows[h * CHUNK : (h + 1) * CHUNK] for h in range(HEADS_STEP)], 1
                )

            q = stack(q_all)
            do = stack(do_all)
            keys = kwin[:width, :]
            values = vwin[:width, :]
            scores = (dot_t(q, keys) * SCALE_LOG2).reshape(HEADS_STEP, CHUNK, width) + bias
            scores = scores.reshape(ROWS_STEP, width)
            highest = jnp.max(scores, axis=-1, keepdims=True)
            powers = jnp.exp2(scores - highest)
            total = jnp.sum(powers, axis=-1, keepdims=True)
            probabilities = powers * (1.0 / total)
            weights = probabilities.astype(BF16)
            attended = dot(weights, values).astype(BF16)
            delta = jnp.sum(do.astype(F32) * attended.astype(F32), axis=-1, keepdims=True)
            slopes = (probabilities * (dot_t(do, values) - delta)).astype(BF16)
            odq_ref[:, span] = unstack(attended)
            odq_ref[:, other] = unstack((dot(slopes, keys) * SCALE).astype(BF16))
            dwin[:HEAD_DIM, :width] = dot(q.astype(F32).T.astype(BF16), slopes)
            dwin[HEAD_DIM:, :width] = dot(do.astype(F32).T.astype(BF16), weights)
            return carry

        block(0, 0)
        back = dwin[:, :width].T
        for t in range(skipped, REACH + 1):
            at = (t - skipped) * CHUNK
            acc[t % RING, unit(t)] += back[at : at + CHUNK, :]

    for index, chunks in enumerate(CLASSES):
        fits = needed <= chunks
        if index == 0:
            fits = needed > CLASSES[1]
        elif index + 1 < len(CLASSES):
            fits = fits & (needed > CLASSES[index + 1])
        pl.when(fits)(functools.partial(run, chunks))

    @pl.when(step == ROW - 1)
    def _():
        for slot in range(RING):
            whole = acc[slot]
            dkv_refs[slot][:, :, :HEAD_DIM] = (whole[:, :, :HEAD_DIM] * SCALE).astype(BF16)
            dkv_refs[slot][:, :, HEAD_DIM:] = whole[:, :, HEAD_DIM:].astype(BF16)


def attention(place, lengths, qdo, slots, v4):
    rows = pl.BlockSpec((CHUNK, 2 * WIDE), lambda i, *_: (i, 0))

    def whole(shape):
        return pl.BlockSpec(shape, lambda i, *_: (0, 0, 0))

    pair = (UNITS, CHUNK, 2 * HEAD_DIM)
    single = (UNITS, CHUNK, HEAD_DIM)
    shapes = [single if slot == RING // 2 else pair for slot in range(RING)] + [single]
    kv_specs = [whole(shape) for shape in shapes]
    big = jax.ShapeDtypeStruct((ROW * CHUNK, 2 * WIDE), BF16)
    return pl.pallas_call(
        attention_kernel,
        out_shape=[big] + [jax.ShapeDtypeStruct(pair, BF16)] * RING,
        grid_spec=pltpu.PrefetchScalarGridSpec(
            num_scalar_prefetch=2,
            grid=(ROW,),
            in_specs=[rows] + kv_specs,
            out_specs=[rows] + [whole(pair)] * RING,
            scratch_shapes=[
                pltpu.VMEM((WINDOW, HEAD_DIM), BF16),
                pltpu.VMEM((WINDOW, HEAD_DIM), BF16),
                pltpu.VMEM((2 * HEAD_DIM, WINDOW), F32),
                pltpu.VMEM((RING, UNITS, CHUNK, 2 * HEAD_DIM), F32),
            ],
        ),
        compiler_params=pltpu.CompilerParams(vmem_limit_bytes=56 * 1024 * 1024),
    )(place, lengths, qdo, *slots, v4)


def around(value, step):
    return lax.ppermute(value, "z", [(i, (i + step) % RING) for i in range(RING)])


def exchanged(value):
    return lax.all_to_all(value, HEAD_AXES, split_axis=0, concat_axis=0, tiled=True)


def split_kernel(a_ref, b_ref, out_ref):
    width = out_ref.shape[2] // 2
    for g in range(out_ref.shape[0]):
        out_ref[g, :, :width] = a_ref[:, g * width : (g + 1) * width]
        out_ref[g, :, width:] = b_ref[:, g * width : (g + 1) * width]


def split_heads(a, b, steps):
    rows, width = a.shape[0], a.shape[1] // KV_HEADS
    count = KV_HEADS // steps
    part = pl.BlockSpec((rows, count * width), lambda g: (0, g))
    return pl.pallas_call(
        split_kernel,
        out_shape=jax.ShapeDtypeStruct((KV_HEADS, rows, 2 * width), a.dtype),
        grid=(steps,),
        in_specs=[part, part],
        out_specs=pl.BlockSpec((count, rows, 2 * width), lambda g: (g, 0, 0)),
    )(a, b)


def merge_kernel(in_ref, a_ref, b_ref):
    width = in_ref.shape[2] // 2
    for g in range(in_ref.shape[0]):
        a_ref[:, g * width : (g + 1) * width] = in_ref[g, :, :width]
        b_ref[:, g * width : (g + 1) * width] = in_ref[g, :, width:]


def merge_heads(value, steps):
    groups, rows, width = value.shape[0], value.shape[1], value.shape[2] // 2
    count = groups // steps
    part = pl.BlockSpec((rows, count * width), lambda g: (0, g))
    whole = jax.ShapeDtypeStruct((rows, groups * width), value.dtype)
    return pl.pallas_call(
        merge_kernel,
        out_shape=[whole, whole],
        grid=(steps,),
        in_specs=[pl.BlockSpec((count, rows, 2 * width), lambda g: (g, 0, 0))],
        out_specs=[part, part],
    )(value)


def added(a, b):
    return (a.astype(F32) + b.astype(F32)).astype(BF16)


def body(queries, key_vectors, value_vectors, output_cotangent, doc_lengths):
    local = key_vectors.shape[0]
    tokens = KV_HEADS * local
    own = exchanged(split_heads(key_vectors, value_vectors, 1)).reshape(tokens, 2 * HEAD_DIM)
    qdo = exchanged(split_heads(queries, output_cotangent, 2)).reshape(tokens, 2 * WIDE)
    half = 2 * CHUNK
    earlier = lax.ppermute(own[half:], "y", [(i, i + 1) for i in range(ROW - 1)])
    units = jnp.concatenate([earlier, own], axis=0)
    middle = RING // 2
    slots = [None] * RING
    slots[0] = units
    up = down = units
    for step in range(1, middle):
        up, down = around(up, 1), around(down, -1)
        slots[RING - step], slots[step] = up, down
    up, down, qdo = lax.optimization_barrier((up, down, qdo))
    slots[middle] = around(up[:, :HEAD_DIM], 1)
    last_values = around(down[:, HEAD_DIM:], -1)
    place = jnp.stack([lax.axis_index("y"), lax.axis_index("z")]).astype(jnp.int32)
    slots = [s.reshape(UNITS, CHUNK, -1) for s in slots]
    results = attention(
        place, doc_lengths, qdo, slots, last_values.reshape(UNITS, CHUNK, HEAD_DIM)
    )
    odq = exchanged(results[0].reshape(KV_HEADS, local, 2 * WIDE))
    parts = [r.reshape(UNITS * CHUNK, -1) for r in results[1:]]
    up = added(parts[middle - 1], around(parts[middle], 1))
    down = parts[middle + 1]
    for step in range(middle - 2, 0, -1):
        up = added(parts[step], around(up, 1))
        down = added(parts[RING - step], around(down, -1))
    mine = parts[0].astype(F32) + around(up, 1).astype(F32) + around(down, -1).astype(F32)
    returned = lax.ppermute(mine[:half].astype(BF16), "y", [(i, i - 1) for i in range(1, ROW)])
    total = jnp.concatenate([mine[half : 2 * half], mine[2 * half :] + returned.astype(F32)], 0)
    total = total.astype(BF16).reshape(KV_HEADS, local, 2 * HEAD_DIM)
    total, odq = lax.optimization_barrier((total, odq))
    attended, query_slope = merge_heads(odq, 2)
    slopes = jnp.swapaxes(exchanged(total), 0, 1)
    key_slope = slopes[:, :, :HEAD_DIM].reshape(local, KV_HEADS * HEAD_DIM)
    value_slope = slopes[:, :, HEAD_DIM:].reshape(local, KV_HEADS * HEAD_DIM)
    return attended, query_slope, key_slope, value_slope


def solution(mesh):
    split = Mesh(mesh.devices.reshape(ROW, ROW, RING, 2), ("y", "x", "z", "core"))
    rows = P(("y", "x", "z", "core"), None)
    return jax.shard_map(
        body,
        mesh=split,
        in_specs=(rows, rows, rows, rows, P()),
        out_specs=(rows, rows, rows, rows),
        check_vma=False,
    )
```

```python
import functools
import math

import jax
import jax.numpy as jnp
from jax import lax
from jax.experimental import pallas as pl
from jax.experimental.pallas import tpu as pltpu
from jax.sharding import Mesh, PartitionSpec as P

HEAD_DIM = 128
KV_HEADS = 8
GROUP = 16
NDOC = 16
CHUNK = 64
RING = 8
ROW = 4
UNITS = ROW + 2
REACH = 16
WINDOW = (REACH + 1) * CHUNK
CLASSES = (17, 14, 12, 10, 8, 6, 4)
HEADS_STEP = 16
ROWS_STEP = HEADS_STEP * CHUNK
MASK_FILL = -1e30
SCALE = 1.0 / math.sqrt(HEAD_DIM)
SCALE_LOG2 = SCALE * math.log2(math.e)
BF16 = jnp.bfloat16
F32 = jnp.float32
HEAD_AXES = ("x", "core")
WIDE = GROUP * HEAD_DIM


def dot_t(a, b):
    return lax.dot_general(a, b, (((1,), (1,)), ((), ())), preferred_element_type=F32)


def dot(a, b):
    return jnp.dot(a, b, preferred_element_type=F32)


def attention_kernel(place, lengths, qdo_ref, *refs):
    kv_refs = refs[:RING]
    v4_ref = refs[RING]
    odq_ref = refs[RING + 1]
    dkv_refs = refs[RING + 2 : 2 * RING + 2]
    kwin, vwin, dwin, acc = refs[2 * RING + 2 :]
    step = pl.program_id(0)
    z = place[1]
    first = ((place[0] * ROW + step) * RING + z) * CHUNK
    base = first - REACH * CHUNK

    @pl.when(step == 0)
    def _():
        acc[...] = jnp.zeros_like(acc)

    def unit(t):
        return step + t // RING + (z + t % RING >= RING).astype(jnp.int32)

    tokens = first + lax.broadcasted_iota(jnp.int32, (CHUNK, 1), 0)
    starts = jnp.zeros((CHUNK, 1), jnp.int32)
    ending = jnp.int32(0)
    earliest = jnp.int32(0)
    for d in range(NDOC):
        ending = ending + lengths[d]
        starts = jnp.where(tokens >= ending, ending, starts)
        earliest = jnp.where(first >= ending, ending, earliest)
    needed = REACH + 1 - (earliest - base) // CHUNK

    def run(chunks):
        skipped = REACH + 1 - chunks
        width = chunks * CHUNK
        for t in range(skipped, REACH + 1):
            at = (t - skipped) * CHUNK
            slot = t % RING
            if slot == RING // 2:
                kwin[at : at + CHUNK, :] = kv_refs[slot][unit(t)]
                vwin[at : at + CHUNK, :] = v4_ref[unit(t)]
            else:
                pair = kv_refs[slot][unit(t)]
                kwin[at : at + CHUNK, :] = pair[:, :HEAD_DIM]
                vwin[at : at + CHUNK, :] = pair[:, HEAD_DIM:]
        columns = base + skipped * CHUNK + lax.broadcasted_iota(jnp.int32, (CHUNK, width), 1)
        allowed = (columns >= starts) & (columns <= tokens)
        bias = jnp.where(allowed, 0.0, MASK_FILL).astype(F32)[None]
        def block(number, carry):
            lanes = pl.multiple_of(number * (HEADS_STEP * HEAD_DIM), HEADS_STEP * HEAD_DIM)
            span = pl.ds(lanes, HEADS_STEP * HEAD_DIM)
            other = pl.ds(WIDE + lanes, HEADS_STEP * HEAD_DIM)
            q_all = qdo_ref[:, span]
            do_all = qdo_ref[:, other]

            def stack(block_all):
                return jnp.concatenate(
                    [block_all[:, h * HEAD_DIM : (h + 1) * HEAD_DIM] for h in range(HEADS_STEP)], 0
                )

            def unstack(rows):
                return jnp.concatenate(
                    [rows[h * CHUNK : (h + 1) * CHUNK] for h in range(HEADS_STEP)], 1
                )

            q = stack(q_all)
            do = stack(do_all)
            keys = kwin[:width, :]
            values = vwin[:width, :]
            scores = (dot_t(q, keys) * SCALE_LOG2).reshape(HEADS_STEP, CHUNK, width) + bias
            scores = scores.reshape(ROWS_STEP, width)
            highest = jnp.max(scores, axis=-1, keepdims=True)
            powers = jnp.exp2(scores - highest)
            total = jnp.sum(powers, axis=-1, keepdims=True)
            probabilities = powers * (1.0 / total)
            weights = probabilities.astype(BF16)
            attended = dot(weights, values).astype(BF16)
            delta = jnp.sum(do.astype(F32) * attended.astype(F32), axis=-1, keepdims=True)
            slopes = (probabilities * (dot_t(do, values) - delta)).astype(BF16)
            odq_ref[:, span] = unstack(attended)
            odq_ref[:, other] = unstack((dot(slopes, keys) * SCALE).astype(BF16))
            dwin[:HEAD_DIM, :width] = dot(q.astype(F32).T.astype(BF16), slopes)
            dwin[HEAD_DIM:, :width] = dot(do.astype(F32).T.astype(BF16), weights)
            return carry

        block(0, 0)
        back = dwin[:, :width].T
        for t in range(skipped, REACH + 1):
            at = (t - skipped) * CHUNK
            acc[t % RING, unit(t)] += back[at : at + CHUNK, :]

    for index, chunks in enumerate(CLASSES):
        fits = needed <= chunks
        if index == 0:
            fits = needed > CLASSES[1]
        elif index + 1 < len(CLASSES):
            fits = fits & (needed > CLASSES[index + 1])
        pl.when(fits)(functools.partial(run, chunks))

    @pl.when(step == ROW - 1)
    def _():
        for slot in range(RING):
            whole = acc[slot]
            dkv_refs[slot][:, :, :HEAD_DIM] = (whole[:, :, :HEAD_DIM] * SCALE).astype(BF16)
            dkv_refs[slot][:, :, HEAD_DIM:] = whole[:, :, HEAD_DIM:].astype(BF16)


def attention(place, lengths, qdo, slots, v4):
    rows = pl.BlockSpec((CHUNK, 2 * WIDE), lambda i, *_: (i, 0))

    def whole(shape):
        return pl.BlockSpec(shape, lambda i, *_: (0, 0, 0))

    pair = (UNITS, CHUNK, 2 * HEAD_DIM)
    single = (UNITS, CHUNK, HEAD_DIM)
    shapes = [single if slot == RING // 2 else pair for slot in range(RING)] + [single]
    kv_specs = [whole(shape) for shape in shapes]
    big = jax.ShapeDtypeStruct((ROW * CHUNK, 2 * WIDE), BF16)
    return pl.pallas_call(
        attention_kernel,
        out_shape=[big] + [jax.ShapeDtypeStruct(pair, BF16)] * RING,
        grid_spec=pltpu.PrefetchScalarGridSpec(
            num_scalar_prefetch=2,
            grid=(ROW,),
            in_specs=[rows] + kv_specs,
            out_specs=[rows] + [whole(pair)] * RING,
            scratch_shapes=[
                pltpu.VMEM((WINDOW, HEAD_DIM), BF16),
                pltpu.VMEM((WINDOW, HEAD_DIM), BF16),
                pltpu.VMEM((2 * HEAD_DIM, WINDOW), F32),
                pltpu.VMEM((RING, UNITS, CHUNK, 2 * HEAD_DIM), F32),
            ],
        ),
        compiler_params=pltpu.CompilerParams(vmem_limit_bytes=56 * 1024 * 1024),
    )(place, lengths, qdo, *slots, v4)


def around(value, step):
    return lax.ppermute(value, "z", [(i, (i + step) % RING) for i in range(RING)])


def to_earlier(value, step):
    pairs = [
        (y * RING + z, (y - 1) * RING + (z + step) % RING)
        for y in range(1, ROW)
        for z in range(RING)
    ]
    return lax.ppermute(value, ("y", "z"), pairs)


def exchanged(value):
    return lax.all_to_all(value, HEAD_AXES, split_axis=0, concat_axis=0, tiled=True)


def split_kernel(a_ref, b_ref, out_ref):
    width = out_ref.shape[2] // 2
    for g in range(out_ref.shape[0]):
        out_ref[g, :, :width] = a_ref[:, g * width : (g + 1) * width]
        out_ref[g, :, width:] = b_ref[:, g * width : (g + 1) * width]


def split_heads(a, b, steps):
    rows, width = a.shape[0], a.shape[1] // KV_HEADS
    count = KV_HEADS // steps
    part = pl.BlockSpec((rows, count * width), lambda g: (0, g))
    return pl.pallas_call(
        split_kernel,
        out_shape=jax.ShapeDtypeStruct((KV_HEADS, rows, 2 * width), a.dtype),
        grid=(steps,),
        in_specs=[part, part],
        out_specs=pl.BlockSpec((count, rows, 2 * width), lambda g: (g, 0, 0)),
    )(a, b)


def merge_kernel(in_ref, a_ref, b_ref):
    width = in_ref.shape[2] // 2
    for g in range(in_ref.shape[0]):
        a_ref[:, g * width : (g + 1) * width] = in_ref[g, :, :width]
        b_ref[:, g * width : (g + 1) * width] = in_ref[g, :, width:]


def merge_heads(value, steps):
    groups, rows, width = value.shape[0], value.shape[1], value.shape[2] // 2
    count = groups // steps
    part = pl.BlockSpec((rows, count * width), lambda g: (0, g))
    whole = jax.ShapeDtypeStruct((rows, groups * width), value.dtype)
    return pl.pallas_call(
        merge_kernel,
        out_shape=[whole, whole],
        grid=(steps,),
        in_specs=[pl.BlockSpec((count, rows, 2 * width), lambda g: (g, 0, 0))],
        out_specs=[part, part],
    )(value)


def added(a, b):
    return (a.astype(F32) + b.astype(F32)).astype(BF16)


def body(queries, key_vectors, value_vectors, output_cotangent, doc_lengths):
    local = key_vectors.shape[0]
    tokens = KV_HEADS * local
    own = exchanged(split_heads(key_vectors, value_vectors, 1)).reshape(tokens, 2 * HEAD_DIM)
    qdo = exchanged(split_heads(queries, output_cotangent, 2)).reshape(tokens, 2 * WIDE)
    half = 2 * CHUNK
    earlier = lax.ppermute(own[half:], "y", [(i, i + 1) for i in range(ROW - 1)])
    units = jnp.concatenate([earlier, own], axis=0)
    middle = RING // 2
    slots = [None] * RING
    slots[0] = units
    up = down = units
    for step in range(1, middle):
        up, down = around(up, 1), around(down, -1)
        slots[RING - step], slots[step] = up, down
    up, down, qdo = lax.optimization_barrier((up, down, qdo))
    slots[middle] = around(up[:, :HEAD_DIM], 1)
    last_values = around(down[:, HEAD_DIM:], -1)
    place = jnp.stack([lax.axis_index("y"), lax.axis_index("z")]).astype(jnp.int32)
    slots = [s.reshape(UNITS, CHUNK, -1) for s in slots]
    results = attention(
        place, doc_lengths, qdo, slots, last_values.reshape(UNITS, CHUNK, HEAD_DIM)
    )
    odq = exchanged(results[0].reshape(KV_HEADS, local, 2 * WIDE))
    parts = [r.reshape(UNITS * CHUNK, -1) for r in results[1:]]
    up = added(parts[middle - 1], around(parts[middle], 1))
    down = parts[middle + 1]
    for step in range(middle - 2, 0, -1):
        up = added(parts[step], around(up, 1))
        down = added(parts[RING - step], around(down, -1))
    up, early = lax.optimization_barrier((up, parts[0][:half]))
    arrivals = [lax.ppermute(early, "y", [(i, i - 1) for i in range(1, ROW)])]
    arrivals += [to_earlier(up[:half], 1), to_earlier(down[:half], -1)]
    total = parts[0][half:].astype(F32)
    total = total + around(up[half:], 1).astype(F32) + around(down[half:], -1).astype(F32)
    returned = sum(value.astype(F32) for value in arrivals)
    total = total + jnp.pad(returned, ((half, 0), (0, 0)))
    total = total.astype(BF16).reshape(KV_HEADS, local, 2 * HEAD_DIM)
    total, odq = lax.optimization_barrier((total, odq))
    attended, query_slope = merge_heads(odq, 2)
    slopes = jnp.swapaxes(exchanged(total), 0, 1)
    key_slope = slopes[:, :, :HEAD_DIM].reshape(local, KV_HEADS * HEAD_DIM)
    value_slope = slopes[:, :, HEAD_DIM:].reshape(local, KV_HEADS * HEAD_DIM)
    return attended, query_slope, key_slope, value_slope


def solution(mesh):
    split = Mesh(mesh.devices.reshape(ROW, ROW, RING, 2), ("y", "x", "z", "core"))
    rows = P(("y", "x", "z", "core"), None)
    return jax.shard_map(
        body,
        mesh=split,
        in_specs=(rows, rows, rows, rows, P()),
        out_specs=(rows, rows, rows, rows),
        check_vma=False,
    )
```
